512 devices in a mesh: leaf: 8 (over z), rows: 64 (over y, x, core).
Axes of the slice: x: 4, y: 8, z: 8, core: 2. Of those that a mesh axis runs over, the one named last changes fastest.
Arguments:
- right_side: float32 [64, 196608], P(None, ('leaf', 'rows')), may hold values from -6 to 6
- tip_tags: int32 [196608], P(('leaf', 'rows')), may hold values from 0 to 2
- leaf_blocks: bfloat16 [3, 384, 196608], P(None, None, ('leaf', 'rows')), may hold values from -0.1875 to 0.1875
- leaf_cols: int32 [512, 2], P(('leaf', 'rows')), may hold values from 0 to 63
- u_panels: bfloat16 [3, 256, 196608], P(None, None, ('leaf', 'rows')), may hold values from -0.375 to 0.375
- v_panels: bfloat16 [3, 256, 196608], P(None, None, ('leaf', 'rows')), may hold values from -0.0390625 to 0.0390625
- cap_top: bfloat16 [2, 256, 512], replicated, may hold values from -0.25 to 0.25
- cap_mid: bfloat16 [4, 256, 512], replicated, may hold values from -0.25 to 0.25
- cap_low: bfloat16 [8, 256, 512], P('leaf'), may hold values from -0.25 to 0.25
Outputs:
- solution: float32 [64, 196608], P(None, ('leaf', 'rows'))
The draws below stay inside these ranges and needn't reach their ends.
All inputs are finite; a program needn't handle non-finite values.
Results may differ from the reference program's by a relative error of at most 0.019.
Values may be sent and summed in bfloat16 or wider, within the bound.
No kernel may reach another device: no remote copies, remote signals or barrier semaphores. Data moves between devices by JAX's collectives and lax.ppermute only.
A program may use at most 128 MiB of HBM per device.

```python
import jax
import jax.numpy as jnp

ROWS_DEV = 384
NRHS = 64
RANK = 256
NNZ = 3
LEVELS = 3
SUB = 64
TOTAL = 196608
DEVICES = 512


def set_ends(result, rng, smallest, largest):
    index_at = [jax.random.randint(jax.random.fold_in(rng, axis), (), 0, length) for axis, length in enumerate(result.shape)]
    main_axis = result.shape.index(max(result.shape))
    next_to = index_at[:main_axis] + [(index_at[main_axis] + 1) % result.shape[main_axis]] + index_at[main_axis + 1:]
    return result.at[tuple(index_at)].set(smallest).at[tuple(next_to)].set(largest)


def levels(stream_key, dims, pieces, smallest, largest):
    def one(axis_at, blocks):
        heights = jax.random.uniform(jax.random.fold_in(jax.random.fold_in(stream_key, 6), axis_at), (blocks,), jnp.float32, smallest / len(pieces), largest / len(pieces))
        return jnp.repeat(jnp.exp(heights), dims[axis_at] // blocks).reshape((-1,) + (1,) * (len(dims) - axis_at - 1))

    gain = one(*pieces[0])
    for cut in pieces[1:]:
        gain = gain * one(*cut)
    return gain


def noise(key, dims, width, most, cuts=(), kind=jnp.bfloat16):
    entries = width * jax.random.normal(key, dims, jnp.float32)
    if cuts:
        entries = entries * levels(key, dims, cuts, -0.22, 0.18)
    return jnp.clip(entries, -most, most).astype(kind)


def setup_inputs(seed: int = 0) -> dict:
    arg_keys = jax.random.split(jax.random.key(seed), 10)
    right_side = noise(arg_keys[0], (NRHS, TOTAL), 1.0, 6.0, ((1, 512),), jnp.float32)
    tip_tags = set_ends(jax.random.randint(arg_keys[1], (TOTAL,), 0, 3), jax.random.fold_in(arg_keys[1], 1), 0, 2).astype(jnp.int32)
    leaf_blocks = noise(arg_keys[2], (NNZ, ROWS_DEV, TOTAL), (NNZ * ROWS_DEV) ** -0.5, 0.1875, ((2, 512),))
    leaf_cols = set_ends(jax.random.randint(arg_keys[3], (DEVICES, NNZ - 1), 0, SUB), jax.random.fold_in(arg_keys[3], 1), 0, SUB - 1).astype(jnp.int32)
    u_panels = noise(arg_keys[4], (LEVELS, RANK, TOTAL), RANK ** -0.5, 0.375, ((2, 512),))
    v_panels = noise(arg_keys[5], (LEVELS, RANK, TOTAL), (TOTAL // 8) ** -0.5, 0.0390625, ((2, 512),))
    cap_top = noise(arg_keys[6], (2, RANK, 2 * RANK), (2 * RANK) ** -0.5, 0.25)
    cap_mid = noise(arg_keys[7], (4, RANK, 2 * RANK), (2 * RANK) ** -0.5, 0.25)
    cap_low = noise(arg_keys[8], (8, RANK, 2 * RANK), (2 * RANK) ** -0.5, 0.25, ((0, 8),))
    return dict(right_side=right_side, tip_tags=tip_tags, leaf_blocks=leaf_blocks, leaf_cols=leaf_cols, u_panels=u_panels, v_panels=v_panels, cap_top=cap_top, cap_mid=cap_mid, cap_low=cap_low)


def tip_factor(tip_tags):
    return jnp.where(tip_tags == 1, 0.6, jnp.where(tip_tags == 2, 1.8, 1.0)).astype(jnp.float32)


def reference(right_side, tip_tags, leaf_blocks, leaf_cols, u_panels, v_panels, cap_top, cap_mid, cap_low):
    total = right_side.shape[1]
    blocks_all = total // ROWS_DEV
    scaled = (right_side * tip_factor(tip_tags)[None, :]).astype(jnp.bfloat16)
    rhs_blocks = scaled.reshape(NRHS, blocks_all, ROWS_DEV).astype(jnp.float32)
    own_block = jnp.arange(blocks_all, dtype=jnp.int32)
    base_block = (own_block // SUB) * SUB
    field = jnp.zeros((NRHS, blocks_all, ROWS_DEV), jnp.float32)
    for slot in range(NNZ):
        grid = leaf_blocks[slot].reshape(ROWS_DEV, blocks_all, ROWS_DEV).astype(jnp.float32)
        if slot == 0:
            chosen = rhs_blocks
        else:
            target = (base_block + leaf_cols[:, slot - 1].astype(jnp.int32)).astype(jnp.int32)
            chosen = jnp.take(rhs_blocks, target, axis=1)
        field = field + jnp.einsum('nbj,jbi->nbi', chosen, grid)
    field = field.reshape(NRHS, total)
    caps = (cap_top, cap_mid, cap_low)
    for height in range(LEVELS):
        count = 2 ** (height + 1)
        span = total // count
        rounded = field.astype(jnp.bfloat16).reshape(NRHS, count, span).astype(jnp.float32)
        v_here = v_panels[height].reshape(RANK, count, span).astype(jnp.float32)
        coeffs = jnp.einsum('ncm,rcm->cnr', rounded, v_here).astype(jnp.bfloat16)
        paired = coeffs.reshape(count // 2, 2, NRHS, RANK)
        stacked = jnp.concatenate([paired[:, 1], paired[:, 0]], axis=2)
        stacked = jnp.repeat(stacked, 2, axis=0).astype(jnp.float32)
        mixed = jnp.einsum('cnk,crk->cnr', stacked, caps[height].astype(jnp.float32)).astype(jnp.bfloat16)
        u_here = u_panels[height].reshape(RANK, count, span).astype(jnp.float32)
        update = jnp.einsum('cnr,rcm->ncm', mixed.astype(jnp.float32), u_here)
        field = field - update.reshape(NRHS, total)
    return field
```

```python
import jax
import jax.numpy as jnp
from jax import lax
from jax.sharding import PartitionSpec as P

NNZ = 3
LEVELS = 3
LANES = 128


def tip_factor(tip_tags):
    return jnp.where(tip_tags == 1, 0.6, jnp.where(tip_tags == 2, 1.8, 1.0)).astype(jnp.float32)


def dot_nt(a, b):
    return lax.dot_general(a, b, (((1,), (1,)), ((), ())), preferred_element_type=jnp.float32)


def swap(value, step, count):
    return lax.ppermute(value, "leaf", [(i, i ^ step) for i in range(count)])


def exchange(value, axis):
    return lax.all_to_all(value, axis, 0, 0, tiled=True)


def shards(
    right_side, tip_tags, leaf_blocks, leaf_cols, u_panels, v_panels, cap_top, cap_mid, cap_low
):
    nrhs, width = right_side.shape
    rank = u_panels.shape[1]
    rows = lax.axis_size("rows")
    leaves = lax.axis_size("leaf")
    leaf_pos = lax.axis_index("leaf")
    share = rank // rows
    bf16 = jnp.bfloat16

    scaled = (right_side * tip_factor(tip_tags)[None, :]).astype(bf16)

    w_first = dot_nt(u_panels[0], v_panels[1:].reshape(2 * rank, width))
    w_second = dot_nt(u_panels[1], v_panels[2])
    w_part = jnp.concatenate([w_first, w_second], axis=1).astype(bf16).reshape(rows, share, 3 * rank)

    columns = jnp.pad(leaf_cols.astype(bf16), ((0, 0), (0, LANES - 2)))
    extra = jnp.concatenate(
        [
            scaled.reshape(rows, width // LANES, LANES),
            jnp.broadcast_to(columns[None], (rows, 1, LANES)),
        ],
        axis=1,
    )
    first = exchange(jnp.concatenate([w_part, extra], axis=2), "rows")
    w_sum = jnp.sum(first[:, :, : 3 * rank].astype(jnp.float32), axis=0)
    table = first[:, : width // LANES, 3 * rank :].reshape(rows, width)
    wanted = first[:, width // LANES, 3 * rank : 3 * rank + 2].astype(jnp.int32)

    hot = (wanted[:, :, None] == jnp.arange(rows, dtype=jnp.int32)).astype(bf16)
    picked = jnp.dot(hot.reshape(rows * 2, rows), table, preferred_element_type=jnp.float32).astype(bf16)
    second = exchange(picked.reshape(rows, 2, width), "rows")

    w_bf = w_sum.astype(bf16)
    w_other = swap(w_bf, 1, leaves)
    upper = (leaf_pos % 2) == 1
    pair = (w_sum[:, :rank] + w_other[:, :rank].astype(jnp.float32)).astype(bf16)
    pair_other = swap(pair, 2, leaves)
    pair_upper = ((leaf_pos // 2) % 2) == 1
    mid = lax.dynamic_index_in_dim(cap_mid, leaf_pos // 2, 0, keepdims=False)
    low = cap_low[0]
    top = lax.dynamic_index_in_dim(cap_top, leaf_pos // 4, 0, keepdims=False)

    def stack(mine, other, is_upper):
        return jnp.concatenate(
            [jnp.where(is_upper, mine, other), jnp.where(is_upper, other, mine)], axis=1
        )

    x_mid = dot_nt(stack(pair, pair_other, pair_upper), mid)
    later = stack(
        jnp.concatenate([w_bf[:, rank : 2 * rank], w_bf[:, 2 * rank :]], axis=0),
        jnp.concatenate([w_other[:, rank : 2 * rank], w_other[:, 2 * rank :]], axis=0),
        upper,
    )
    x_low = dot_nt(later, low)
    x_rows = jnp.concatenate([x_mid, x_low[:share], x_low[share:]], axis=1).astype(bf16)

    blocks = jnp.concatenate([scaled, second[:, 0], second[:, 1]], axis=1)
    field = jnp.dot(
        blocks, leaf_blocks.reshape(NNZ * width, width), preferred_element_type=jnp.float32
    )
    partial = dot_nt(field.astype(bf16), v_panels.reshape(LEVELS * rank, width)).astype(bf16)

    third = exchange(
        jnp.concatenate(
            [
                partial.reshape(rows, 2, 3 * rank // 2),
                jnp.broadcast_to(x_rows.reshape(1, 2, 6 * rank), (rows, 2, 6 * rank)),
            ],
            axis=2,
        ),
        "rows",
    )
    own = jnp.sum(third[:, :, : 3 * rank // 2].astype(jnp.float32), axis=0).reshape(1, 1, 3 * rank)
    x_all = third[:, :, 3 * rank // 2 :].reshape(rank, 3 * rank)

    every = exchange(jnp.broadcast_to(own, (leaves, 1, 3 * rank)), "leaf").reshape(leaves, LEVELS, rank)
    halves = every[:, 0].reshape(2, leaves // 2, rank).sum(axis=1)
    pairs = every[:, 1].reshape(leaves // 2, 2, rank).sum(axis=1)
    pairs = lax.dynamic_slice_in_dim(pairs, leaf_pos // 4 * 2, 2, 0)
    singles = lax.dynamic_slice_in_dim(every[:, 2], leaf_pos // 2 * 2, 2, 0)

    def coupled(both, cap):
        stacked = jnp.concatenate([both[1:2], both[0:1]], axis=1).astype(bf16)
        return dot_nt(stacked, cap)

    mixed_top = coupled(halves, top).astype(bf16)
    from_top = jnp.dot(mixed_top, x_all[:, : 2 * rank], preferred_element_type=jnp.float32)
    mixed_mid = (coupled(pairs, mid) - from_top[:, :rank]).astype(bf16)
    from_mid = jnp.dot(mixed_mid, x_all[:, 2 * rank :], preferred_element_type=jnp.float32)
    mixed_low = (coupled(singles, low) - from_top[:, rank:] - from_mid).astype(bf16)
    mixed = jnp.concatenate([mixed_top, mixed_mid, mixed_low], axis=1)

    last = exchange(jnp.broadcast_to(mixed[None], (rows, 1, 3 * rank)), "rows").reshape(nrhs, 3 * rank)
    return field - jnp.dot(
        last, u_panels.reshape(LEVELS * rank, width), preferred_element_type=jnp.float32
    )


def solution(mesh):
    placed = (
        P(None, ("leaf", "rows")),
        P(("leaf", "rows")),
        P(None, None, ("leaf", "rows")),
        P(("leaf", "rows"), None),
        P(None, None, ("leaf", "rows")),
        P(None, None, ("leaf", "rows")),
        P(),
        P(),
        P("leaf", None, None),
    )
    return jax.shard_map(
        shards, mesh=mesh, in_specs=placed, out_specs=P(None, ("leaf", "rows")), check_vma=False
    )
```

```python
import jax
import jax.numpy as jnp
from jax import lax
from jax.sharding import PartitionSpec as P

NNZ = 3
LEVELS = 3
LANES = 128


def tip_factor(tip_tags):
    return jnp.where(tip_tags == 1, 0.6, jnp.where(tip_tags == 2, 1.8, 1.0)).astype(jnp.float32)


def dot_nt(a, b):
    return lax.dot_general(a, b, (((1,), (1,)), ((), ())), preferred_element_type=jnp.float32)


def swap(value, axis, step):
    return lax.ppermute(value, axis, [(i, i ^ step) for i in range(lax.axis_size(axis))])


def exchange(value, axis):
    return lax.all_to_all(value, axis, 0, 0, tiled=True)


def shards(
    right_side, tip_tags, leaf_blocks, leaf_cols, u_panels, v_panels, cap_top, cap_mid, cap_low
):
    nrhs, width = right_side.shape
    rank = u_panels.shape[1]
    rows = lax.axis_size("rows")
    leaves = lax.axis_size("leaf")
    leaf_pos = lax.axis_index("leaf")
    core = lax.axis_index("rows") % 2
    share = rank // rows
    half = share // 2
    bf16 = jnp.bfloat16

    scaled = (right_side * tip_factor(tip_tags)[None, :]).astype(bf16)

    w_first = dot_nt(u_panels[0], v_panels[1:].reshape(2 * rank, width))
    w_second = dot_nt(u_panels[1], v_panels[2])
    w_part = jnp.concatenate([w_first, w_second], axis=1).astype(bf16)
    w_part = w_part.reshape(2, rows, half, 3 * rank).swapaxes(0, 1).reshape(rows, share, 3 * rank)

    columns = jnp.pad(leaf_cols.astype(bf16), ((0, 0), (0, LANES - 2)))
    extra = jnp.concatenate(
        [
            scaled.reshape(rows, width // LANES, LANES),
            jnp.broadcast_to(columns[None], (rows, 1, LANES)),
        ],
        axis=1,
    )
    first = exchange(jnp.concatenate([w_part, extra], axis=2), "rows")
    w_sum = jnp.sum(first[:, :, : 3 * rank].astype(jnp.float32), axis=0)
    table = first[:, : width // LANES, 3 * rank :].reshape(rows, width)
    wanted = first[:, width // LANES, 3 * rank : 3 * rank + 2].astype(jnp.int32)

    hot = (wanted[:, :, None] == jnp.arange(rows, dtype=jnp.int32)).astype(bf16)
    picked = jnp.dot(hot.reshape(rows * 2, rows), table, preferred_element_type=jnp.float32).astype(bf16)
    second = exchange(picked.reshape(rows, 2, width), "rows")

    w_bf, picked = lax.optimization_barrier((w_sum.astype(bf16), picked))
    w_other = swap(w_bf, "leaf", 1)
    upper = (leaf_pos % 2) == 1
    pair = (w_sum[:, :rank] + w_other[:, :rank].astype(jnp.float32)).astype(bf16)
    pair_other = swap(pair, "leaf", 2)
    pair_upper = ((leaf_pos // 2) % 2) == 1
    mid = lax.dynamic_index_in_dim(cap_mid, leaf_pos // 2, 0, keepdims=False)
    low = cap_low[0]
    top = lax.dynamic_index_in_dim(cap_top, leaf_pos // 4, 0, keepdims=False)

    def stack(mine, other, is_upper):
        return jnp.concatenate(
            [jnp.where(is_upper, mine, other), jnp.where(is_upper, other, mine)], axis=1
        )

    x_mid = dot_nt(stack(pair, pair_other, pair_upper), mid)
    later = stack(
        jnp.concatenate([w_bf[:, rank : 2 * rank], w_bf[:, 2 * rank :]], axis=0),
        jnp.concatenate([w_other[:, rank : 2 * rank], w_other[:, 2 * rank :]], axis=0),
        upper,
    )
    x_low = dot_nt(later, low)
    x_rows = jnp.concatenate([x_mid, x_low[:share], x_low[share:]], axis=1).astype(bf16)

    blocks = jnp.concatenate([scaled, second[:, 0], second[:, 1]], axis=1)
    field = jnp.dot(
        blocks, leaf_blocks.reshape(NNZ * width, width), preferred_element_type=jnp.float32
    )
    partial = dot_nt(field.astype(bf16), v_panels.reshape(LEVELS * rank, width)).astype(bf16)

    x_half = jnp.broadcast_to(x_rows.reshape(1, 2, half, 3 * rank), (rows // 2, 2, half, 3 * rank))
    third = exchange(
        jnp.concatenate(
            [
                partial.reshape(rows, half, 3 * rank // half),
                x_half.reshape(rows, half, 3 * rank),
            ],
            axis=2,
        ),
        "rows",
    )
    own = jnp.sum(third[:, :, : 3 * rank // half].astype(jnp.float32), axis=0).astype(bf16)
    x_mine = third[:, :, 3 * rank // half :].reshape(rank // 2, 3 * rank)
    x_theirs = swap(x_mine, "rows", 1)

    every = exchange(jnp.broadcast_to(own[None], (leaves,) + own.shape), "leaf")
    every = every.reshape(leaves, LEVELS, rank).astype(jnp.float32)
    halves = every[:, 0].reshape(2, leaves // 2, rank).sum(axis=1)
    pairs = every[:, 1].reshape(leaves // 2, 2, rank).sum(axis=1)
    pairs = lax.dynamic_slice_in_dim(pairs, leaf_pos // 4 * 2, 2, 0)
    singles = lax.dynamic_slice_in_dim(every[:, 2], leaf_pos // 2 * 2, 2, 0)

    def coupled(both, cap):
        stacked = jnp.concatenate([both[1:2], both[0:1]], axis=1).astype(bf16)
        return dot_nt(stacked, cap)

    def through(mixed, at):
        lower, upper_half = mixed[:, : rank // 2], mixed[:, rank // 2 :]
        mine = jnp.where(core == 1, upper_half, lower)
        theirs = jnp.where(core == 1, lower, upper_half)
        return jnp.dot(mine, x_mine[:, at], preferred_element_type=jnp.float32) + jnp.dot(
            theirs, x_theirs[:, at], preferred_element_type=jnp.float32
        )

    mixed_top = coupled(halves, top).astype(bf16)
    from_top = through(mixed_top, slice(0, 2 * rank))
    mixed_mid = (coupled(pairs, mid) - from_top[:, :rank]).astype(bf16)
    from_mid = through(mixed_mid, slice(2 * rank, 3 * rank))
    mixed_low = (coupled(singles, low) - from_top[:, rank:] - from_mid).astype(bf16)
    mixed = jnp.concatenate([mixed_top, mixed_mid, mixed_low], axis=1)

    mixed = mixed.reshape(1, 2, 3 * rank // 2)
    last = exchange(jnp.broadcast_to(mixed, (rows,) + mixed.shape[1:]), "rows").reshape(nrhs, 3 * rank)
    return field - jnp.dot(
        last, u_panels.reshape(LEVELS * rank, width), preferred_element_type=jnp.float32
    )


def solution(mesh):
    placed = (
        P(None, ("leaf", "rows")),
        P(("leaf", "rows")),
        P(None, None, ("leaf", "rows")),
        P(("leaf", "rows"), None),
        P(None, None, ("leaf", "rows")),
        P(None, None, ("leaf", "rows")),
        P(),
        P(),
        P("leaf", None, None),
    )
    return jax.shard_map(
        shards, mesh=mesh, in_specs=placed, out_specs=P(None, ("leaf", "rows")), check_vma=False
    )
```

```python
import jax
import jax.numpy as jnp
from jax import lax
from jax.sharding import PartitionSpec as P

NNZ = 3
LEVELS = 3
LANES = 128
CORES = 2


def tip_factor(tip_tags):
    return jnp.where(tip_tags == 1, 0.6, jnp.where(tip_tags == 2, 1.8, 1.0)).astype(jnp.float32)


def dot(a, b):
    return jnp.dot(a, b, preferred_element_type=jnp.float32)


def dot_nt(a, b):
    return lax.dot_general(a, b, (((1,), (1,)), ((), ())), preferred_element_type=jnp.float32)


def swap_cores(value):
    return lax.ppermute(value, "rows", [(i, i ^ 1) for i in range(lax.axis_size("rows"))])


def exchange(value, axis):
    return lax.all_to_all(value, axis, 0, 0, tiled=True)


def shards(
    right_side, tip_tags, leaf_blocks, leaf_cols, u_panels, v_panels, cap_top, cap_mid, cap_low
):
    nrhs, width = right_side.shape
    rank = u_panels.shape[1]
    half = rank // CORES
    wide = LEVELS * rank
    rows = lax.axis_size("rows")
    leaves = lax.axis_size("leaf")
    leaf_pos = lax.axis_index("leaf")
    second_core = lax.axis_index("rows") % CORES == 1
    bf16 = jnp.bfloat16

    def mine_theirs(lower, upper):
        return jnp.where(second_core, upper, lower), jnp.where(second_core, lower, upper)

    scaled = (right_side * tip_factor(tip_tags)[None, :]).astype(bf16)

    columns = jnp.pad(leaf_cols.astype(bf16), ((0, 0), (0, LANES - 2)))
    own_rows = jnp.concatenate(
        [
            scaled.reshape(rows, width // LANES, LANES),
            jnp.broadcast_to(columns[None], (rows, 1, LANES)),
        ],
        axis=1,
    )
    first = exchange(own_rows, "rows")
    table = first[:, : width // LANES].reshape(rows, width)
    wanted = first[:, width // LANES, :2].astype(jnp.int32)

    u_here, v_here, _ = lax.optimization_barrier((u_panels, v_panels, own_rows))
    w_first = dot_nt(u_here[0], v_here[1:].reshape(2 * rank, width))
    w_second = dot_nt(u_here[1], v_here[2])
    w_all = jnp.concatenate([w_first, w_second], axis=1).astype(bf16)
    w_mine, w_theirs = mine_theirs(w_all[:half], w_all[half:])
    w_chip = (w_mine.astype(jnp.float32) + swap_cores(w_theirs).astype(jnp.float32)).astype(bf16)

    hot = (wanted[:, :, None] == jnp.arange(rows, dtype=jnp.int32)).astype(bf16)
    picked = dot(hot.reshape(rows * 2, rows), table).astype(bf16)
    second = exchange(picked.reshape(rows, 2, width), "rows")

    blocks = jnp.concatenate([scaled, second[:, 0], second[:, 1]], axis=1)
    field = dot(blocks, leaf_blocks.reshape(NNZ * width, width))
    partial = dot_nt(field.astype(bf16), v_panels.reshape(wide, width)).astype(bf16)

    third = exchange(
        jnp.concatenate(
            [partial.reshape(rows, 2, wide // 2), w_chip.reshape(rows, half // rows, wide)], axis=2
        ),
        "rows",
    )
    third = third.reshape(rows // CORES, CORES, 2, 3 * wide // 2).astype(jnp.float32).sum(axis=0)
    own = third[:, :, : wide // 2].sum(axis=0)
    w_rows = third[:, :, wide // 2 :].reshape(CORES, 2 * wide)

    fourth = exchange(
        jnp.broadcast_to(
            jnp.concatenate([own, w_rows], axis=1).astype(bf16)[None], (leaves, 2, 5 * wide // 2)
        ),
        "leaf",
    ).astype(jnp.float32)
    every = fourth[:, :, : wide // 2].reshape(leaves, LEVELS, rank)
    w_every = fourth[:, :, wide // 2 :].reshape(leaves, 4, wide)

    def two_of(value, first_one):
        return lax.dynamic_slice_in_dim(value, first_one, 2, 0)

    def coupled(both, cap):
        return dot_nt(jnp.concatenate([both[1], both[0]], axis=1).astype(bf16), cap)

    top = lax.dynamic_index_in_dim(cap_top, leaf_pos // 4, 0, keepdims=False)
    mid = lax.dynamic_index_in_dim(cap_mid, leaf_pos // 2, 0, keepdims=False)
    low = cap_low[0]
    halves = every[:, 0].reshape(2, leaves // 2, 1, rank).sum(axis=1)
    mid_in = jnp.concatenate([every[:, 1:2], w_every[:, :, :rank]], axis=1)
    mid_in = two_of(mid_in.reshape(leaves // 2, 2, 5, rank).sum(axis=1), leaf_pos // 4 * 2)
    low_in = jnp.concatenate(
        [every[:, 2:3], w_every[:, :, rank : 2 * rank], w_every[:, :, 2 * rank :]], axis=1
    )
    low_in = two_of(low_in, leaf_pos // 2 * 2)
    top_out = coupled(halves, top)
    mid_out = coupled(mid_in, mid)
    low_out = coupled(low_in, low)
    start = jnp.concatenate([top_out, mid_out[:1], low_out[:1]], axis=1).astype(bf16)
    x_rows = jnp.concatenate([mid_out[1:], low_out[1:5], low_out[5:]], axis=1).astype(bf16)

    x_half = jnp.broadcast_to(x_rows.reshape(1, CORES, 2, wide), (rows // CORES, CORES, 2, wide))
    fifth = exchange(
        jnp.concatenate(
            [
                jnp.broadcast_to(start.reshape(1, 2, wide // 2), (rows, 2, wide // 2)),
                x_half.reshape(rows, 2, wide),
            ],
            axis=2,
        ),
        "rows",
    )
    x_mine = fifth[:, :, wide // 2 :].reshape(half, wide)
    x_theirs = swap_cores(x_mine)
    start = fifth[:, :, : wide // 2].reshape(nrhs, wide)
    mixed_top = start[:, :rank]

    def through(mixed, at):
        mine, theirs = mine_theirs(mixed[:, :half], mixed[:, half:])
        return dot(mine, x_mine[:, at]) + dot(theirs, x_theirs[:, at])

    from_top = through(mixed_top, slice(0, 2 * rank))
    mixed_mid = (start[:, rank : 2 * rank].astype(jnp.float32) - from_top[:, :rank]).astype(bf16)
    from_mid = through(mixed_mid, slice(2 * rank, wide))
    mixed_low = (start[:, 2 * rank :].astype(jnp.float32) - from_top[:, rank:] - from_mid).astype(bf16)
    mixed = jnp.concatenate([mixed_top, mixed_mid, mixed_low], axis=1)
    return field - dot(mixed, u_panels.reshape(wide, width))


def solution(mesh):
    placed = (
        P(None, ("leaf", "rows")),
        P(("leaf", "rows")),
        P(None, None, ("leaf", "rows")),
        P(("leaf", "rows"), None),
        P(None, None, ("leaf", "rows")),
        P(None, None, ("leaf", "rows")),
        P(),
        P(),
        P("leaf", None, None),
    )
    return jax.shard_map(
        shards, mesh=mesh, in_specs=placed, out_specs=P(None, ("leaf", "rows")), check_vma=False
    )
```

```python
import jax
import jax.numpy as jnp
from jax import lax
from jax.sharding import Mesh
from jax.sharding import PartitionSpec as P

NNZ = 3
LEVELS = 3
LANES = 128
CORES = 2
ROWS = ("chip", "core")
ALL = ("leaf",) + ROWS


def tip_factor(tip_tags):
    return jnp.where(tip_tags == 1, 0.6, jnp.where(tip_tags == 2, 1.8, 1.0)).astype(jnp.float32)


def dot(a, b):
    return jnp.dot(a, b, preferred_element_type=jnp.float32)


def dot_nt(a, b):
    return lax.dot_general(a, b, (((1,), (1,)), ((), ())), preferred_element_type=jnp.float32)


def swap_cores(value):
    return lax.ppermute(value, "core", [(i, i ^ 1) for i in range(CORES)])


def exchange(value, axis):
    return lax.all_to_all(value, axis, 0, 0, tiled=True)


def shards(
    right_side, tip_tags, leaf_blocks, leaf_cols, u_panels, v_panels, cap_top, cap_mid, cap_low
):
    nrhs, width = right_side.shape
    rank = u_panels.shape[1]
    half = rank // CORES
    wide = LEVELS * rank
    chips = lax.axis_size("chip")
    rows = chips * CORES
    leaves = lax.axis_size("leaf")
    leaf_pos = lax.axis_index("leaf")
    second_core = lax.axis_index("core") == 1
    late_half = leaf_pos // (leaves // 2) == 1
    late_pair = leaf_pos // 2 % 2 == 1
    bf16 = jnp.bfloat16

    def mine_theirs(lower, upper):
        return jnp.where(second_core, upper, lower), jnp.where(second_core, lower, upper)

    scaled = (right_side * tip_factor(tip_tags)[None, :]).astype(bf16)

    columns = jnp.pad(leaf_cols.astype(bf16), ((0, 0), (0, LANES - 2)))
    own_rows = jnp.concatenate(
        [
            scaled.reshape(rows, width // LANES, LANES),
            jnp.broadcast_to(columns[None], (rows, 1, LANES)),
        ],
        axis=1,
    )
    first = exchange(own_rows, ROWS)
    table = first[:, : width // LANES].reshape(rows, width)
    wanted = first[:, width // LANES, :2].astype(jnp.int32)

    u_here, v_here, _ = lax.optimization_barrier((u_panels, v_panels, own_rows))
    w_first = dot_nt(u_here[0], v_here[1:].reshape(2 * rank, width))
    w_second = dot_nt(u_here[1], v_here[2])
    w_all = jnp.concatenate([w_first, w_second], axis=1).astype(bf16)
    w_mine, w_theirs = mine_theirs(w_all[:, : wide // 2], w_all[:, wide // 2 :])

    hot = (wanted[:, :, None] == jnp.arange(rows, dtype=jnp.int32)).astype(bf16)
    picked = dot(hot.reshape(rows * 2, rows), table).astype(bf16)
    top = lax.dynamic_index_in_dim(cap_top, leaf_pos // 4, 0, keepdims=False)
    mid = lax.dynamic_index_in_dim(cap_mid, leaf_pos // 2, 0, keepdims=False)
    top, mid, w_mine, w_theirs = lax.optimization_barrier((top, mid, w_mine, w_theirs))
    w_chip = (w_mine.astype(jnp.float32) + swap_cores(w_theirs).astype(jnp.float32)).astype(bf16)
    picked, late_half, late_pair, second_core = lax.optimization_barrier(
        (picked, late_half, late_pair, second_core)
    )
    second = exchange(picked.reshape(rows, 2, width), ROWS)

    blocks = jnp.concatenate([scaled, second[:, 0], second[:, 1]], axis=1)
    field = dot(blocks, leaf_blocks.reshape(NNZ * width, width))
    partial = dot_nt(field.astype(bf16), v_panels.reshape(wide, width)).astype(bf16)

    w_chip = w_chip.reshape(CORES, chips, rank // rows, wide // 2).swapaxes(0, 1)
    third = exchange(
        jnp.concatenate(
            [partial.reshape(rows, 2, wide // 2), w_chip.reshape(rows, 2, wide)], axis=2
        ),
        ROWS,
    )
    third = third.reshape(chips, CORES, 2, 3 * wide // 2).astype(jnp.float32).sum(axis=0)
    own = third[:, :, : wide // 2].sum(axis=0)
    w_rows = third[:, :, wide // 2 :].reshape(CORES, 2 * wide)

    fourth = exchange(
        jnp.broadcast_to(
            jnp.concatenate([own, w_rows], axis=1).astype(bf16)[None], (leaves, 2, 5 * wide // 2)
        ),
        "leaf",
    ).astype(jnp.float32)
    every = fourth[:, :, : wide // 2].reshape(leaves, LEVELS, rank)
    w_every = fourth[:, :, wide // 2 :].reshape(leaves, CORES, rank // rows, wide // 2)
    w_every = w_every.swapaxes(1, 2).reshape(leaves, rank // rows, wide)

    def part(value, late):
        count = value.shape[0] // 2
        return jnp.where(late, value[count:], value[:count])

    def coupled(both, cap):
        return dot_nt(jnp.concatenate([both[1], both[0]], axis=1).astype(bf16), cap)

    halves = every[:, 0].reshape(2, leaves // 2, 1, rank).sum(axis=1)
    mid_in = jnp.concatenate([every[:, 1:2], w_every[:, :, :rank]], axis=1)
    mid_in = part(mid_in, late_half)
    mid_in = mid_in.reshape(2, 2, mid_in.shape[1], rank).sum(axis=1)
    low_in = jnp.concatenate(
        [every[:, 2:3], w_every[:, :, rank : 2 * rank], w_every[:, :, 2 * rank :]], axis=1
    )
    low_in = part(part(low_in, late_half), late_pair)
    top_out = coupled(halves, top)
    mid_out = coupled(mid_in, mid)
    low_out = coupled(low_in, cap_low[0])
    start = jnp.concatenate([top_out, mid_out[:1], low_out[:1]], axis=1).astype(bf16)
    x_rows = jnp.concatenate([mid_out[1:], low_out[1:5], low_out[5:]], axis=1).astype(bf16)

    message = jnp.concatenate([start.reshape(2, wide // 2), x_rows.reshape(2, 2 * wide)], axis=1)
    fifth_mine = exchange(jnp.broadcast_to(message[None], (chips,) + message.shape), "chip")
    fifth_theirs = swap_cores(fifth_mine)
    x_mine = fifth_mine[:, :, wide // 2 :].reshape(half, wide)
    x_theirs = fifth_theirs[:, :, wide // 2 :].reshape(half, wide)
    start = jnp.stack(
        mine_theirs(fifth_mine[:, :, : wide // 2], fifth_theirs[:, :, : wide // 2]), axis=1
    ).reshape(nrhs, wide)
    mixed_top = start[:, :rank]

    def through(mixed, at):
        mine, theirs = mine_theirs(mixed[:, :half], mixed[:, half:])
        return dot(mine, x_mine[:, at]) + dot(theirs, x_theirs[:, at])

    from_top = through(mixed_top, slice(0, 2 * rank))
    mixed_mid = (start[:, rank : 2 * rank].astype(jnp.float32) - from_top[:, :rank]).astype(bf16)
    from_mid = through(mixed_mid, slice(2 * rank, wide))
    mixed_low = (start[:, 2 * rank :].astype(jnp.float32) - from_top[:, rank:] - from_mid).astype(bf16)
    mixed = jnp.concatenate([mixed_top, mixed_mid, mixed_low], axis=1)
    return field - dot(mixed, u_panels.reshape(wide, width))


def solution(mesh):
    placed = (
        P(None, ALL),
        P(ALL),
        P(None, None, ALL),
        P(ALL, None),
        P(None, None, ALL),
        P(None, None, ALL),
        P(),
        P(),
        P("leaf", None, None),
    )
    leaves, rows = mesh.devices.shape
    split = Mesh(mesh.devices.reshape(leaves, rows // CORES, CORES), ALL)
    return jax.shard_map(
        shards, mesh=split, in_specs=placed, out_specs=P(None, ALL), check_vma=False
    )
```

```python
import jax
import jax.numpy as jnp
from jax import lax
from jax.experimental import pallas as pl
from jax.experimental.pallas import tpu as pltpu
from jax.sharding import Mesh
from jax.sharding import PartitionSpec as P

NNZ = 3
LEVELS = 3
LANES = 128
CORES = 2
ROWS = ("chip", "core")
ALL = ("leaf",) + ROWS


def tip_factor(tip_tags):
    return jnp.where(tip_tags == 1, 0.6, jnp.where(tip_tags == 2, 1.8, 1.0)).astype(jnp.float32)


def dot(a, b):
    return jnp.dot(a, b, preferred_element_type=jnp.float32)


def dot_nt(a, b):
    return lax.dot_general(a, b, (((1,), (1,)), ((), ())), preferred_element_type=jnp.float32)


def swap_cores(value):
    return lax.ppermute(value, "core", [(i, i ^ 1) for i in range(CORES)])


def exchange(value, axis):
    return lax.all_to_all(value, axis, 0, 0, tiled=True)


def call(kernel, inputs, scalars, *outputs):
    vmem = pl.BlockSpec(memory_space=pltpu.VMEM)
    smem = pl.BlockSpec(memory_space=pltpu.SMEM)
    return pl.pallas_call(
        kernel,
        out_shape=[jax.ShapeDtypeStruct(*output) for output in outputs],
        in_specs=[smem] * len(scalars) + [vmem] * len(inputs),
        out_specs=[vmem] * len(outputs),
        compiler_params=pltpu.CompilerParams(vmem_limit_bytes=12 * 2**20),
    )(*scalars, *inputs)


def solve_kernel(leaf_ref, fourth_ref, top_ref, mid_ref, low_ref, message_ref):
    leaf_pos = leaf_ref[0, 0]
    leaves = fourth_ref.shape[0]
    rank = top_ref.shape[0]
    edge = LEVELS * rank // 2
    first = fourth_ref[:, 0, :].astype(jnp.float32)
    second = fourth_ref[:, 1, :].astype(jnp.float32)
    every = [
        jnp.concatenate([first[:, at : at + edge], second[:, at : at + edge]], axis=1)
        for at in range(0, first.shape[1], edge)
    ]
    subtree = lax.broadcasted_iota(jnp.int32, (leaves, rank), 0)

    def stacked(value, span):
        parent = leaf_pos // (2 * span) * 2

        def child(which):
            inside = subtree // span == parent + which
            return jnp.sum(jnp.where(inside, value, 0.0), axis=0, keepdims=True)

        return jnp.concatenate([child(1), child(0)], axis=1)

    def coupled(values, span, cap):
        rows = [stacked(value, span) for value in values]
        rows += [jnp.zeros_like(rows[0])] * (-len(rows) % 8)
        return dot_nt(jnp.concatenate(rows, axis=0).astype(jnp.bfloat16), cap)

    def level(value, at):
        return value[:, at * rank : (at + 1) * rank]

    top_out = coupled([level(every[0], 0)], leaves // 2, top_ref[...])
    mid_out = coupled(
        [level(every[0], 1)] + [level(value, 0) for value in every[1:]], leaves // 4, mid_ref[...]
    )
    low_out = coupled(
        [level(every[0], 2)] + [level(value, at) for at in (1, 2) for value in every[1:]],
        leaves // 8,
        low_ref[0],
    )
    count = len(every) - 1
    start = jnp.concatenate([top_out[:1], mid_out[:1], low_out[:1]], axis=1)
    x_rows = [
        jnp.concatenate(
            [mid_out[at : at + 1], low_out[at : at + 1], low_out[at + count : at + count + 1]], axis=1
        )
        for at in range(1, count + 1)
    ]
    for at in range(2):
        row = jnp.concatenate(
            [start[:, at * edge : (at + 1) * edge]] + x_rows[at * count // 2 : (at + 1) * count // 2],
            axis=1,
        ).astype(jnp.bfloat16)
        message_ref[:, at, :] = jnp.broadcast_to(row, (message_ref.shape[0], row.shape[1]))


def shards(
    right_side, tip_tags, leaf_blocks, leaf_cols, u_panels, v_panels, cap_top, cap_mid, cap_low
):
    nrhs, width = right_side.shape
    rank = u_panels.shape[1]
    half = rank // CORES
    wide = LEVELS * rank
    chips = lax.axis_size("chip")
    rows = chips * CORES
    leaves = lax.axis_size("leaf")
    leaf_pos = lax.axis_index("leaf")
    second_core = lax.axis_index("core") == 1
    bf16 = jnp.bfloat16

    def mine_theirs(lower, upper):
        return jnp.where(second_core, upper, lower), jnp.where(second_core, lower, upper)

    scaled = (right_side * tip_factor(tip_tags)[None, :]).astype(bf16)

    columns = jnp.pad(leaf_cols.astype(bf16), ((0, 0), (0, LANES - 2)))
    own_rows = jnp.concatenate(
        [
            scaled.reshape(rows, width // LANES, LANES),
            jnp.broadcast_to(columns[None], (rows, 1, LANES)),
        ],
        axis=1,
    )
    first = exchange(own_rows, ROWS)
    table = first[:, : width // LANES].reshape(rows, width)
    wanted = first[:, width // LANES, :2].astype(jnp.int32)

    u_here, v_here, _ = lax.optimization_barrier((u_panels, v_panels, own_rows))
    w_first = dot_nt(u_here[0], v_here[1:].reshape(2 * rank, width))
    w_second = dot_nt(u_here[1], v_here[2])
    w_all = jnp.concatenate([w_first, w_second], axis=1).astype(bf16)
    w_mine, w_theirs = mine_theirs(w_all[:, : wide // 2], w_all[:, wide // 2 :])

    hot = (wanted[:, :, None] == jnp.arange(rows, dtype=jnp.int32)).astype(bf16)
    picked = dot(hot.reshape(rows * 2, rows), table).astype(bf16)
    top = lax.dynamic_index_in_dim(cap_top, leaf_pos // 4, 0, keepdims=False)
    mid = lax.dynamic_index_in_dim(cap_mid, leaf_pos // 2, 0, keepdims=False)
    top, mid, w_mine, w_theirs = lax.optimization_barrier((top, mid, w_mine, w_theirs))
    w_chip = (w_mine.astype(jnp.float32) + swap_cores(w_theirs).astype(jnp.float32)).astype(bf16)
    picked, second_core = lax.optimization_barrier((picked, second_core))
    second = exchange(picked.reshape(rows, 2, width), ROWS)

    blocks = jnp.concatenate([scaled, second[:, 0], second[:, 1]], axis=1)
    field = dot(blocks, leaf_blocks.reshape(NNZ * width, width))
    partial = dot_nt(field.astype(bf16), v_panels.reshape(wide, width)).astype(bf16)

    w_chip = w_chip.reshape(CORES, chips, rank // rows, wide // 2).swapaxes(0, 1)
    third = exchange(
        jnp.concatenate(
            [partial.reshape(rows, 2, wide // 2), w_chip.reshape(rows, 2, wide)], axis=2
        ),
        ROWS,
    )
    third = third.reshape(chips, CORES, 2, 3 * wide // 2).astype(jnp.float32).sum(axis=0)
    own = third[:, :, : wide // 2].sum(axis=0)
    w_rows = third[:, :, wide // 2 :].reshape(CORES, 2 * wide)

    fourth = exchange(
        jnp.broadcast_to(
            jnp.concatenate([own, w_rows], axis=1).astype(bf16)[None], (leaves, 2, 5 * wide // 2)
        ),
        "leaf",
    )

    (message,) = call(
        solve_kernel,
        (fourth, top, mid, cap_low),
        (leaf_pos.astype(jnp.int32).reshape(1, 1),),
        ((chips, 2, 5 * wide // 2), bf16),
    )
    fifth_mine = exchange(message, "chip")
    fifth_theirs = swap_cores(fifth_mine)
    x_mine = fifth_mine[:, :, wide // 2 :].reshape(half, wide)
    x_theirs = fifth_theirs[:, :, wide // 2 :].reshape(half, wide)
    start = jnp.stack(
        mine_theirs(fifth_mine[:, :, : wide // 2], fifth_theirs[:, :, : wide // 2]), axis=1
    ).reshape(nrhs, wide)
    mixed_top = start[:, :rank]

    def through(mixed, at):
        mine, theirs = mine_theirs(mixed[:, :half], mixed[:, half:])
        return dot(mine, x_mine[:, at]) + dot(theirs, x_theirs[:, at])

    from_top = through(mixed_top, slice(0, 2 * rank))
    mixed_mid = (start[:, rank : 2 * rank].astype(jnp.float32) - from_top[:, :rank]).astype(bf16)
    from_mid = through(mixed_mid, slice(2 * rank, wide))
    mixed_low = (start[:, 2 * rank :].astype(jnp.float32) - from_top[:, rank:] - from_mid).astype(bf16)
    mixed = jnp.concatenate([mixed_top, mixed_mid, mixed_low], axis=1)
    return field - dot(mixed, u_panels.reshape(wide, width))


def solution(mesh):
    placed = (
        P(None, ALL),
        P(ALL),
        P(None, None, ALL),
        P(ALL, None),
        P(None, None, ALL),
        P(None, None, ALL),
        P(),
        P(),
        P("leaf", None, None),
    )
    leaves, rows = mesh.devices.shape
    split = Mesh(mesh.devices.reshape(leaves, rows // CORES, CORES), ALL)
    return jax.shard_map(
        shards, mesh=split, in_specs=placed, out_specs=P(None, ALL), check_vma=False
    )
```

```python
import jax
import jax.numpy as jnp
from jax import lax
from jax.experimental import pallas as pl
from jax.experimental.pallas import tpu as pltpu
from jax.sharding import Mesh
from jax.sharding import PartitionSpec as P

NNZ = 3
LEVELS = 3
LANES = 128
CORES = 2
ROWS = ("chip", "core")
ALL = ("leaf",) + ROWS


def tip_factor(tip_tags):
    return jnp.where(tip_tags == 1, 0.6, jnp.where(tip_tags == 2, 1.8, 1.0)).astype(jnp.float32)


def dot(a, b):
    return jnp.dot(a, b, preferred_element_type=jnp.float32)


def dot_nt(a, b):
    return lax.dot_general(a, b, (((1,), (1,)), ((), ())), preferred_element_type=jnp.float32)


def swap_cores(value):
    return lax.ppermute(value, "core", [(i, i ^ 1) for i in range(CORES)])


def exchange(value, axis):
    return lax.all_to_all(value, axis, 0, 0, tiled=True)


def call(kernel, inputs, scalars, *outputs):
    vmem = pl.BlockSpec(memory_space=pltpu.VMEM)
    smem = pl.BlockSpec(memory_space=pltpu.SMEM)
    return pl.pallas_call(
        kernel,
        out_shape=[jax.ShapeDtypeStruct(*output) for output in outputs],
        in_specs=[smem] * len(scalars) + [vmem] * len(inputs),
        out_specs=[vmem] * len(outputs),
        compiler_params=pltpu.CompilerParams(vmem_limit_bytes=12 * 2**20),
    )(*scalars, *inputs)


def leaf_kernel(scaled_ref, second_ref, leaf_ref, v_ref, w_ref, field_ref, message_ref):
    edge = v_ref.shape[0] // 2
    field = dot(scaled_ref[...], leaf_ref[0])
    for slot in range(NNZ - 1):
        field += dot(second_ref[:, slot, :], leaf_ref[slot + 1])
    field_ref[...] = field
    partial = dot_nt(field.astype(jnp.bfloat16), v_ref[...]).astype(jnp.bfloat16)
    for at in range(2):
        message_ref[:, at, :edge] = partial[:, at * edge : (at + 1) * edge]
    message_ref[:, :, edge:] = w_ref[...]


def solve_kernel(leaf_ref, fourth_ref, top_ref, mid_ref, low_ref, message_ref):
    leaf_pos = leaf_ref[0, 0]
    leaves = fourth_ref.shape[0]
    rank = top_ref.shape[0]
    edge = LEVELS * rank // 2
    first = fourth_ref[:, 0, :].astype(jnp.float32)
    second = fourth_ref[:, 1, :].astype(jnp.float32)
    every = [
        jnp.concatenate([first[:, at : at + edge], second[:, at : at + edge]], axis=1)
        for at in range(0, first.shape[1], edge)
    ]
    subtree = lax.broadcasted_iota(jnp.int32, (leaves, rank), 0)

    def stacked(value, span):
        parent = leaf_pos // (2 * span) * 2

        def child(which):
            inside = subtree // span == parent + which
            return jnp.sum(jnp.where(inside, value, 0.0), axis=0, keepdims=True)

        return jnp.concatenate([child(1), child(0)], axis=1)

    def coupled(values, span, cap):
        rows = [stacked(value, span) for value in values]
        rows += [jnp.zeros_like(rows[0])] * (-len(rows) % 8)
        return dot_nt(jnp.concatenate(rows, axis=0).astype(jnp.bfloat16), cap)

    def level(value, at):
        return value[:, at * rank : (at + 1) * rank]

    top_out = coupled([level(every[0], 0)], leaves // 2, top_ref[...])
    mid_out = coupled(
        [level(every[0], 1)] + [level(value, 0) for value in every[1:]], leaves // 4, mid_ref[...]
    )
    low_out = coupled(
        [level(every[0], 2)] + [level(value, at) for at in (1, 2) for value in every[1:]],
        leaves // 8,
        low_ref[0],
    )
    count = len(every) - 1
    start = jnp.concatenate([top_out[:1], mid_out[:1], low_out[:1]], axis=1)
    x_rows = [
        jnp.concatenate(
            [mid_out[at : at + 1], low_out[at : at + 1], low_out[at + count : at + count + 1]], axis=1
        )
        for at in range(1, count + 1)
    ]
    for at in range(2):
        row = jnp.concatenate(
            [start[:, at * edge : (at + 1) * edge]] + x_rows[at * count // 2 : (at + 1) * count // 2],
            axis=1,
        ).astype(jnp.bfloat16)
        message_ref[:, at, :] = jnp.broadcast_to(row, (message_ref.shape[0], row.shape[1]))


def shards(
    right_side, tip_tags, leaf_blocks, leaf_cols, u_panels, v_panels, cap_top, cap_mid, cap_low
):
    nrhs, width = right_side.shape
    rank = u_panels.shape[1]
    half = rank // CORES
    wide = LEVELS * rank
    chips = lax.axis_size("chip")
    rows = chips * CORES
    leaves = lax.axis_size("leaf")
    leaf_pos = lax.axis_index("leaf")
    second_core = lax.axis_index("core") == 1
    bf16 = jnp.bfloat16

    def mine_theirs(lower, upper):
        return jnp.where(second_core, upper, lower), jnp.where(second_core, lower, upper)

    scaled = (right_side * tip_factor(tip_tags)[None, :]).astype(bf16)

    columns = jnp.pad(leaf_cols.astype(bf16), ((0, 0), (0, LANES - 2)))
    own_rows = jnp.concatenate(
        [
            scaled.reshape(rows, width // LANES, LANES),
            jnp.broadcast_to(columns[None], (rows, 1, LANES)),
        ],
        axis=1,
    )
    first = exchange(own_rows, ROWS)
    table = first[:, : width // LANES].reshape(rows, width)
    wanted = first[:, width // LANES, :2].astype(jnp.int32)

    u_here, v_here, _ = lax.optimization_barrier((u_panels, v_panels, own_rows))
    w_first = dot_nt(u_here[0], v_here[1:].reshape(2 * rank, width))
    w_second = dot_nt(u_here[1], v_here[2])
    w_all = jnp.concatenate([w_first, w_second], axis=1).astype(bf16)
    w_mine, w_theirs = mine_theirs(w_all[:, : wide // 2], w_all[:, wide // 2 :])

    hot = (wanted[:, :, None] == jnp.arange(rows, dtype=jnp.int32)).astype(bf16)
    picked = dot(hot.reshape(rows * 2, rows), table).astype(bf16)
    tops, mids, picked = lax.optimization_barrier((cap_top, cap_mid, picked))
    top = lax.dynamic_index_in_dim(tops, leaf_pos // 4, 0, keepdims=False)
    mid = lax.dynamic_index_in_dim(mids, leaf_pos // 2, 0, keepdims=False)
    w_mine, w_theirs = lax.optimization_barrier((w_mine, w_theirs))
    w_chip = (w_mine.astype(jnp.float32) + swap_cores(w_theirs).astype(jnp.float32)).astype(bf16)
    top, mid, w_chip = lax.optimization_barrier((top, mid, w_chip))
    second = exchange(picked.reshape(rows, 2, width), ROWS)

    w_chip = w_chip.reshape(CORES, chips, rank // rows, wide // 2).swapaxes(0, 1)
    field, message = call(
        leaf_kernel,
        (scaled, second, leaf_blocks, v_panels.reshape(wide, width), w_chip.reshape(rows, 2, wide)),
        (),
        ((nrhs, width), jnp.float32),
        ((rows, 2, 3 * wide // 2), bf16),
    )

    third = exchange(message, ROWS)
    third = third.reshape(chips, CORES, 2, 3 * wide // 2).astype(jnp.float32).sum(axis=0)
    own = third[:, :, : wide // 2].sum(axis=0)
    w_rows = third[:, :, wide // 2 :].reshape(CORES, 2 * wide)

    fourth = exchange(
        jnp.broadcast_to(
            jnp.concatenate([own, w_rows], axis=1).astype(bf16)[None], (leaves, 2, 5 * wide // 2)
        ),
        "leaf",
    )

    (message,) = call(
        solve_kernel,
        (fourth, top, mid, cap_low),
        (leaf_pos.astype(jnp.int32).reshape(1, 1),),
        ((chips, 2, 5 * wide // 2), bf16),
    )
    fifth_mine = exchange(message, "chip")
    fifth_theirs = swap_cores(fifth_mine)
    x_mine = fifth_mine[:, :, wide // 2 :].reshape(half, wide)
    x_theirs = fifth_theirs[:, :, wide // 2 :].reshape(half, wide)
    start = jnp.stack(
        mine_theirs(fifth_mine[:, :, : wide // 2], fifth_theirs[:, :, : wide // 2]), axis=1
    ).reshape(nrhs, wide)
    mixed_top = start[:, :rank]

    def through(mixed, at):
        mine, theirs = mine_theirs(mixed[:, :half], mixed[:, half:])
        return dot(mine, x_mine[:, at]) + dot(theirs, x_theirs[:, at])

    from_top = through(mixed_top, slice(0, 2 * rank))
    mixed_mid = (start[:, rank : 2 * rank].astype(jnp.float32) - from_top[:, :rank]).astype(bf16)
    from_mid = through(mixed_mid, slice(2 * rank, wide))
    mixed_low = (start[:, 2 * rank :].astype(jnp.float32) - from_top[:, rank:] - from_mid).astype(bf16)
    mixed = jnp.concatenate([mixed_top, mixed_mid, mixed_low], axis=1)
    return field - dot(mixed, u_panels.reshape(wide, width))


def solution(mesh):
    placed = (
        P(None, ALL),
        P(ALL),
        P(None, None, ALL),
        P(ALL, None),
        P(None, None, ALL),
        P(None, None, ALL),
        P(),
        P(),
        P("leaf", None, None),
    )
    leaves, rows = mesh.devices.shape
    split = Mesh(mesh.devices.reshape(leaves, rows // CORES, CORES), ALL)
    return jax.shard_map(
        shards, mesh=split, in_specs=placed, out_specs=P(None, ALL), check_vma=False
    )
```

```python
import jax
import jax.numpy as jnp
from jax import lax
from jax.experimental import pallas as pl
from jax.experimental.pallas import tpu as pltpu
from jax.sharding import Mesh
from jax.sharding import PartitionSpec as P

NNZ = 3
LEVELS = 3
LANES = 128
CORES = 2
ROWS = ("chip", "core")
ALL = ("leaf",) + ROWS


def tip_factor(tip_tags):
    return jnp.where(tip_tags == 1, 0.6, jnp.where(tip_tags == 2, 1.8, 1.0)).astype(jnp.float32)


def dot(a, b):
    return jnp.dot(a, b, preferred_element_type=jnp.float32)


def dot_nt(a, b):
    return lax.dot_general(a, b, (((1,), (1,)), ((), ())), preferred_element_type=jnp.float32)


def swap_cores(value):
    return lax.ppermute(value, "core", [(i, i ^ 1) for i in range(CORES)])


def exchange(value, axis):
    return lax.all_to_all(value, axis, 0, 0, tiled=True)


def call(kernel, inputs, scalars, *outputs):
    vmem = pl.BlockSpec(memory_space=pltpu.VMEM)
    smem = pl.BlockSpec(memory_space=pltpu.SMEM)
    return pl.pallas_call(
        kernel,
        out_shape=[jax.ShapeDtypeStruct(*output) for output in outputs],
        in_specs=[smem] * len(scalars) + [vmem] * len(inputs),
        out_specs=[vmem] * len(outputs),
        compiler_params=pltpu.CompilerParams(vmem_limit_bytes=12 * 2**20),
    )(*scalars, *inputs)


def leaf_kernel(scaled_ref, second_ref, leaf_ref, v_ref, w_ref, field_ref, message_ref):
    edge = v_ref.shape[0] // 2
    field = dot(scaled_ref[...], leaf_ref[0])
    for slot in range(NNZ - 1):
        field += dot(second_ref[:, slot, :], leaf_ref[slot + 1])
    field_ref[...] = field
    partial = dot_nt(field.astype(jnp.bfloat16), v_ref[...]).astype(jnp.bfloat16)
    for at in range(2):
        message_ref[:, at, :edge] = partial[:, at * edge : (at + 1) * edge]
    message_ref[:, :, edge:] = w_ref[...]


def solve_kernel(leaf_ref, fourth_ref, top_ref, mid_ref, low_ref, message_ref):
    leaf_pos = leaf_ref[0, 0]
    leaves = fourth_ref.shape[0]
    rank = top_ref.shape[0]
    edge = LEVELS * rank // 2
    first = fourth_ref[:, 0, :].astype(jnp.float32)
    second = fourth_ref[:, 1, :].astype(jnp.float32)
    every = [
        jnp.concatenate([first[:, at : at + edge], second[:, at : at + edge]], axis=1)
        for at in range(0, first.shape[1], edge)
    ]
    subtree = lax.broadcasted_iota(jnp.int32, (leaves, rank), 0)

    def stacked(value, span):
        parent = leaf_pos // (2 * span) * 2

        def child(which):
            inside = subtree // span == parent + which
            return jnp.sum(jnp.where(inside, value, 0.0), axis=0, keepdims=True)

        return jnp.concatenate([child(1), child(0)], axis=1)

    def coupled(values, span, cap):
        rows = [stacked(value, span) for value in values]
        rows += [jnp.zeros_like(rows[0])] * (-len(rows) % 8)
        return dot_nt(jnp.concatenate(rows, axis=0).astype(jnp.bfloat16), cap)

    def level(value, at):
        return value[:, at * rank : (at + 1) * rank]

    top_out = coupled([level(every[0], 0)], leaves // 2, top_ref[...])
    mid_out = coupled(
        [level(every[0], 1)] + [level(value, 0) for value in every[1:]], leaves // 4, mid_ref[...]
    )
    low_out = coupled(
        [level(every[0], 2)] + [level(value, at) for at in (1, 2) for value in every[1:]],
        leaves // 8,
        low_ref[0],
    )
    count = len(every) - 1
    start = jnp.concatenate([top_out[:1], mid_out[:1], low_out[:1]], axis=1)
    x_rows = [
        jnp.concatenate(
            [mid_out[at : at + 1], low_out[at : at + 1], low_out[at + count : at + count + 1]], axis=1
        )
        for at in range(1, count + 1)
    ]
    for at in range(2):
        row = jnp.concatenate(
            [start[:, at * edge : (at + 1) * edge]] + x_rows[at * count // 2 : (at + 1) * count // 2],
            axis=1,
        ).astype(jnp.bfloat16)
        message_ref[:, at, :] = jnp.broadcast_to(row, (message_ref.shape[0], row.shape[1]))


def finish_kernel(core_ref, mine_ref, theirs_ref, field_ref, u_ref, solution_ref):
    second_core = core_ref[0, 0] == 1
    wide = u_ref.shape[0]
    rank = wide // LEVELS
    half = rank // CORES
    edge = wide // 2

    def start_of(ref):
        return jnp.concatenate([ref[:, 0, :edge], ref[:, 1, :edge]], axis=1).astype(jnp.float32)

    def x_of(ref):
        return ref[:, :, edge:].astype(jnp.float32).reshape(half, wide).astype(jnp.bfloat16)

    x_mine, x_theirs = x_of(mine_ref), x_of(theirs_ref)
    start_mine, start_theirs = start_of(mine_ref), start_of(theirs_ref)
    first = jnp.where(second_core, start_theirs, start_mine)
    second = jnp.where(second_core, start_mine, start_theirs)
    start = jnp.stack([first, second], axis=1).reshape(2 * first.shape[0], wide)

    def through(mixed, at):
        lower, upper = mixed[:, :half], mixed[:, half:]
        mine = jnp.where(second_core, upper, lower).astype(jnp.bfloat16)
        theirs = jnp.where(second_core, lower, upper).astype(jnp.bfloat16)
        return dot(mine, x_mine[:, at]) + dot(theirs, x_theirs[:, at])

    from_top = through(start[:, :rank], slice(0, 2 * rank))
    mixed_mid = start[:, rank : 2 * rank] - from_top[:, :rank]
    from_mid = through(mixed_mid, slice(2 * rank, wide))
    mixed_low = start[:, 2 * rank :] - from_top[:, rank:] - from_mid
    mixed = jnp.concatenate([start[:, :rank], mixed_mid, mixed_low], axis=1).astype(jnp.bfloat16)
    solution_ref[...] = field_ref[...] - dot(mixed, u_ref[...])


def shards(
    right_side, tip_tags, leaf_blocks, leaf_cols, u_panels, v_panels, cap_top, cap_mid, cap_low
):
    nrhs, width = right_side.shape
    rank = u_panels.shape[1]
    wide = LEVELS * rank
    chips = lax.axis_size("chip")
    rows = chips * CORES
    leaves = lax.axis_size("leaf")
    leaf_pos = lax.axis_index("leaf")
    second_core = lax.axis_index("core") == 1
    bf16 = jnp.bfloat16

    def mine_theirs(lower, upper):
        return jnp.where(second_core, upper, lower), jnp.where(second_core, lower, upper)

    scaled = (right_side * tip_factor(tip_tags)[None, :]).astype(bf16)

    columns = jnp.pad(leaf_cols.astype(bf16), ((0, 0), (0, LANES - 2)))
    own_rows = jnp.concatenate(
        [
            scaled.reshape(rows, width // LANES, LANES),
            jnp.broadcast_to(columns[None], (rows, 1, LANES)),
        ],
        axis=1,
    )
    first = exchange(own_rows, ROWS)
    table = first[:, : width // LANES].reshape(rows, width)
    wanted = first[:, width // LANES, :2].astype(jnp.int32)

    u_here, v_here, _ = lax.optimization_barrier((u_panels, v_panels, own_rows))
    w_first = dot_nt(u_here[0], v_here[1:].reshape(2 * rank, width))
    w_second = dot_nt(u_here[1], v_here[2])
    w_all = jnp.concatenate([w_first, w_second], axis=1).astype(bf16)
    w_mine, w_theirs = mine_theirs(w_all[:, : wide // 2], w_all[:, wide // 2 :])

    hot = (wanted[:, :, None] == jnp.arange(rows, dtype=jnp.int32)).astype(bf16)
    picked = dot(hot.reshape(rows * 2, rows), table).astype(bf16)
    tops, mids, picked = lax.optimization_barrier((cap_top, cap_mid, picked))
    top = lax.dynamic_index_in_dim(tops, leaf_pos // 4, 0, keepdims=False)
    mid = lax.dynamic_index_in_dim(mids, leaf_pos // 2, 0, keepdims=False)
    w_mine, w_theirs = lax.optimization_barrier((w_mine, w_theirs))
    w_chip = (w_mine.astype(jnp.float32) + swap_cores(w_theirs).astype(jnp.float32)).astype(bf16)
    top, mid, w_chip = lax.optimization_barrier((top, mid, w_chip))
    second = exchange(picked.reshape(rows, 2, width), ROWS)

    w_chip = w_chip.reshape(CORES, chips, rank // rows, wide // 2).swapaxes(0, 1)
    field, message = call(
        leaf_kernel,
        (scaled, second, leaf_blocks, v_panels.reshape(wide, width), w_chip.reshape(rows, 2, wide)),
        (),
        ((nrhs, width), jnp.float32),
        ((rows, 2, 3 * wide // 2), bf16),
    )

    third = exchange(message, ROWS)
    third = third.reshape(chips, CORES, 2, 3 * wide // 2).astype(jnp.float32).sum(axis=0)
    own = third[:, :, : wide // 2].sum(axis=0)
    w_rows = third[:, :, wide // 2 :].reshape(CORES, 2 * wide)

    fourth = exchange(
        jnp.broadcast_to(
            jnp.concatenate([own, w_rows], axis=1).astype(bf16)[None], (leaves, 2, 5 * wide // 2)
        ),
        "leaf",
    )

    (message,) = call(
        solve_kernel,
        (fourth, top, mid, cap_low),
        (leaf_pos.astype(jnp.int32).reshape(1, 1),),
        ((chips, 2, 5 * wide // 2), bf16),
    )
    fifth_mine = exchange(message, "chip")
    fifth_theirs = swap_cores(fifth_mine)
    (result,) = call(
        finish_kernel,
        (fifth_mine, fifth_theirs, field, u_panels.reshape(wide, width)),
        (lax.axis_index("core").astype(jnp.int32).reshape(1, 1),),
        ((nrhs, width), jnp.float32),
    )
    return result


def solution(mesh):
    placed = (
        P(None, ALL),
        P(ALL),
        P(None, None, ALL),
        P(ALL, None),
        P(None, None, ALL),
        P(None, None, ALL),
        P(),
        P(),
        P("leaf", None, None),
    )
    leaves, rows = mesh.devices.shape
    split = Mesh(mesh.devices.reshape(leaves, rows // CORES, CORES), ALL)
    return jax.shard_map(
        shards, mesh=split, in_specs=placed, out_specs=P(None, ALL), check_vma=False
    )
```
